256 devices in a mesh: freq: 16 (over x, y), clus: 16 (over z, core).
Axes of the slice: x: 4, y: 4, z: 8, core: 2. Of those that a mesh axis runs over, the one named last changes fastest.
Arguments:
- history: bfloat16 [1024, 8, 2048], P('freq', None, 'clus'), may hold values from -6 to 6
- near_blocks: bfloat16 [16, 4, 512, 2, 128, 128], P('clus', None, 'freq'), may hold values from -0.1875 to 0.1875
- near_list: int32 [16, 4], replicated, may hold values from 0 to 15, as said below
- basis_out: bfloat16 [512, 2, 32, 2048], P('freq', None, None, 'clus'), may hold values from -0.75 to 0.75
- basis_in: bfloat16 [512, 2, 32, 2048], P('freq', None, None, 'clus'), may hold values from -0.375 to 0.375
- coupling: bfloat16 [16, 512, 2, 32, 512], P('clus', 'freq'), may hold values from -0.25 to 0.25
- ranks: int32 [16, 512, 16], P('clus', 'freq'), may hold values from 4 to 32
Outputs:
- potential: bfloat16 [512, 2, 8, 2048], P('freq', None, None, 'clus')
The draws below stay inside these ranges and needn't reach their ends.
Inputs may be any that keep to these rules, and one draw needn't show every extreme that they name: `near_list`: row t starts with t itself; its other 3 entries are distinct shards other than t, each (t + d) mod 16 for some d with 1 <= |d| <= 3.
All inputs are finite; a program needn't handle non-finite values.
Results may differ from the reference program's by a relative error of at most 0.0055.
Values may be sent and summed in bfloat16 or wider, within the bound.
No kernel may reach another device: no remote copies, remote signals or barrier semaphores. Data moves between devices by JAX's collectives and lax.ppermute only.
A program may use at most 128 MiB of HBM per device.

```python
import math
import jax
import jax.numpy as jnp
from jax import lax

STEPS = 1024
WAVES = 512
EXC = 8
PC = 128
NEAR = 4
RANK = 32
NPAN = 2048
N_CLUS = 16


def draw_near_list(key, part):
    reach = NEAR - 1

    def one_row(target):
        order = jax.random.permutation(jax.random.fold_in(key, target), 2 * reach)[:reach].astype(jnp.int32)
        offsets = jnp.where(order < reach, order + 1, reach - 1 - order)
        others = (target + offsets + N_CLUS) % N_CLUS
        return jnp.concatenate([jnp.reshape(target, (1,)).astype(jnp.int32), others.astype(jnp.int32)])
    return jax.vmap(one_row)(lax.iota(jnp.int32, N_CLUS))


def place_ends(drawn, own_key, smallest, top_value):
    longest = drawn.shape.index(max(drawn.shape))
    spots = []
    for shift in (0, 1):
        where = [jax.random.randint(jax.random.fold_in(own_key, axis), (), 0, length) for axis, length in enumerate(drawn.shape)]
        where[longest] = (where[longest] + shift) % drawn.shape[longest]
        spots.append(tuple(where))
    return drawn.at[spots[0]].set(smallest).at[spots[1]].set(top_value)


def shard_levels(stream_key, dims, pieces, least, largest):
    gain = 1.0
    for axis_at, blocks in pieces:
        draws = jax.random.uniform(jax.random.fold_in(jax.random.fold_in(stream_key, 6), axis_at), (blocks,), jnp.float32, least / len(pieces), largest / len(pieces))
        gain = gain * jnp.repeat(jnp.exp(draws), dims[axis_at] // blocks).reshape((-1,) + (1,) * (len(dims) - 1 - axis_at))
    return gain


def centred(rng, extent, deviation, most, cuts=(), held_as=jnp.bfloat16):
    entries = deviation * jax.random.normal(rng, extent, jnp.float32)
    if cuts:
        entries = entries * shard_levels(rng, extent, cuts, -0.22, 0.18)
    return jnp.clip(entries, -most, most).astype(held_as)


def setup_inputs(seed: int = 0) -> dict:
    arg_keys = jax.random.split(jax.random.key(seed), 8)
    return {
        "history": centred(arg_keys[0], (STEPS, EXC, NPAN), 1.0, 6.0, ((0, 16), (2, 16))),
        "near_blocks": centred(arg_keys[1], (N_CLUS, NEAR, WAVES, 2, PC, PC), (2 * NEAR * PC) ** -0.5, 0.1875, ((0, 16), (2, 16))),
        "near_list": draw_near_list(jax.random.fold_in(arg_keys[7], 71), 0),
        "basis_out": centred(arg_keys[3], (WAVES, 2, RANK, NPAN), (2 * RANK) ** -0.5, 0.75, ((0, 16), (3, 16))),
        "basis_in": centred(arg_keys[4], (WAVES, 2, RANK, NPAN), (2 * PC) ** -0.5, 0.375, ((0, 16), (3, 16))),
        "coupling": centred(arg_keys[5], (N_CLUS, WAVES, 2, RANK, N_CLUS * RANK), (RANK * N_CLUS) ** -0.5, 0.25, ((0, 16), (1, 16))),
        "ranks": place_ends(jax.random.randint(arg_keys[6], (N_CLUS, WAVES, N_CLUS), RANK // 8, RANK + 1), jax.random.fold_in(arg_keys[6], 1), RANK // 8, RANK).astype(jnp.int32),
    }


def wave_table(first_wave, count, first_step, length, total):
    waves = first_wave + lax.iota(jnp.int32, count)
    steps = first_step + lax.iota(jnp.int32, length)
    phase = (waves[:, None] * steps[None, :]) % total
    angle = phase.astype(jnp.float32) * (2.0 * math.pi / total)
    weight = jnp.exp(steps.astype(jnp.float32) * (-math.log(2.0) / total)) * (total ** -0.5)
    return weight[None, :] * jnp.cos(angle), -weight[None, :] * jnp.sin(angle)


def transform(history, cos_tab, sin_tab):
    flat = history.reshape(history.shape[0], -1).astype(jnp.float32)
    real_part = jnp.dot(cos_tab, flat, precision=lax.Precision.HIGHEST)
    imag_part = jnp.dot(sin_tab, flat, precision=lax.Precision.HIGHEST)
    return jnp.stack([real_part, imag_part], 1).reshape(cos_tab.shape[0], 2, history.shape[1], history.shape[2])


def complex_product(form, left_re, left_im, right_re, right_im):
    def product(left, right):
        return jnp.einsum(form, left.astype(jnp.float32), right.astype(jnp.float32))
    return product(left_re, right_re) - product(left_im, right_im), product(left_re, right_im) + product(left_im, right_re)


def far_mask(limit, nearby, clusters, rank):
    position = lax.iota(jnp.int32, rank)
    keep_out = position[None, None, :] < limit[:, :, None]
    keep_in = keep_out & jnp.logical_not(nearby)[None, :, None]
    mask = jnp.transpose(keep_out, (0, 2, 1))[:, :, :, None] & keep_in[:, None, :, :]
    return mask.reshape(limit.shape[0], rank, clusters * rank)


def reference(history, near_blocks, near_list, basis_out, basis_in, coupling, ranks):
    cos_tab, sin_tab = wave_table(0, WAVES, 0, STEPS, STEPS)
    dens = transform(history, cos_tab, sin_tab).astype(jnp.bfloat16)
    spaced = dens.reshape(WAVES, 2, EXC, N_CLUS, PC)
    basis = basis_in.reshape(WAVES, 2, RANK, N_CLUS, PC)
    coeff_re, coeff_im = complex_product("krsp,kesp->kesr", basis[:, 0], basis[:, 1], spaced[:, 0], spaced[:, 1])
    coeffs = jnp.stack([coeff_re, coeff_im], 1).astype(jnp.bfloat16)
    stacked = coeffs.reshape(WAVES, 2, EXC, N_CLUS * RANK)
    cluster_ids = lax.iota(jnp.int32, N_CLUS)
    outputs = []
    for target in range(N_CLUS):
        chosen = jnp.stack([lax.dynamic_slice_in_dim(dens, (near_list[target, slot] * PC).astype(jnp.int32), PC, 3) for slot in range(NEAR)])
        blocks = near_blocks[target]
        near_re, near_im = complex_product("jkpq,jkeq->kep", blocks[:, :, 0], blocks[:, :, 1], chosen[:, :, 0], chosen[:, :, 1])
        nearby = jnp.any(near_list[target][:, None] == cluster_ids[None, :], axis=0)
        mask = far_mask(ranks[target], nearby, N_CLUS, RANK)
        couple = coupling[target]
        couple_re = jnp.where(mask, couple[:, 0], jnp.zeros_like(couple[:, 0]))
        couple_im = jnp.where(mask, couple[:, 1], jnp.zeros_like(couple[:, 1]))
        mixed_re, mixed_im = complex_product("kim,kem->kei", couple_re, couple_im, stacked[:, 0], stacked[:, 1])
        mixed_re = mixed_re.astype(jnp.bfloat16)
        mixed_im = mixed_im.astype(jnp.bfloat16)
        out_basis = basis_out[:, :, :, target * PC:(target + 1) * PC]
        far_re, far_im = complex_product("kip,kei->kep", out_basis[:, 0], out_basis[:, 1], mixed_re, mixed_im)
        outputs.append(jnp.stack([near_re + far_re, near_im + far_im], 1).astype(jnp.bfloat16))
    return jnp.concatenate(outputs, axis=3)
```

```python
import math

import jax
import jax.numpy as jnp
from jax import lax
from jax.experimental import pallas as pl
from jax.experimental.pallas import tpu as pltpu
from jax.sharding import PartitionSpec as P

STEPS = 1024
F32 = jnp.float32
BF16 = jnp.bfloat16
VMEM = pltpu.VMEM
OFFSETS = (1, -1, 2, -2, 3, -3)


def params(mib=48):
    return pltpu.CompilerParams(vmem_limit_bytes=mib * 1024 * 1024)


def nt(a, b):
    return lax.dot_general(a, b, (((1,), (1,)), ((), ())), preferred_element_type=F32)


def nn(a, b):
    return lax.dot_general(a, b, (((1,), (0,)), ((), ())), preferred_element_type=F32)


def tn(a, b):
    return lax.dot_general(a, b, (((0,), (0,)), ((), ())), preferred_element_type=F32)


def from_behind(block, axis, distance):
    devices = range(lax.axis_size(axis))
    route = [((i - distance) % len(devices), i) for i in devices]
    return lax.ppermute(block, axis, route)


def pack_kernel(hist_ref, out_ref):
    exc = hist_ref.shape[1]
    slabs = jnp.swapaxes(hist_ref[...].astype(F32), 0, 1).astype(BF16)
    for copy in range(out_ref.shape[0] // exc):
        out_ref[copy * exc : (copy + 1) * exc] = slabs


def table_kernel(half_ref, hi_ref, lo_ref, base_c, base_s):
    dests, waves, lanes = 8, 32, 128
    count = dests * waves
    first = half_ref[0] * count
    wave = first + lax.broadcasted_iota(jnp.int32, (count, lanes), 0)
    step = lax.broadcasted_iota(jnp.int32, (count, lanes), 1)
    theta = lax.rem(wave * step, STEPS).astype(F32) * (2.0 * math.pi / STEPS)
    weight = jnp.exp(step.astype(F32) * (-math.log(2.0) / STEPS)) * STEPS ** (-0.5)
    base_c[...] = weight * jnp.cos(theta)
    base_s[...] = weight * jnp.sin(theta)
    sub = lax.broadcasted_iota(jnp.int32, (8, lanes), 0)
    for block in range(STEPS // lanes):
        gain = 2.0 ** (-block * lanes / STEPS)
        for part in range(2):
            phi = ((sub * block + 2 * part) & 7).astype(F32) * (math.pi / 4.0)
            turn_c = (gain * jnp.cos(phi))[None]
            turn_s = (gain * jnp.sin(phi))[None]
            for dest in range(dests):
                rows = slice(dest * waves, (dest + 1) * waves)
                tc = base_c[rows].reshape(waves // 8, 8, lanes)
                ts = base_s[rows].reshape(waves // 8, 8, lanes)
                value = (tc * turn_c - ts * turn_s).reshape(waves, lanes)
                hi = value.astype(BF16)
                lo = (value - hi.astype(F32)).astype(BF16)
                to = slice((dest * 2 + part) * waves, (dest * 2 + part + 1) * waves)
                hi_ref[to, block * lanes : (block + 1) * lanes] = hi
                lo_ref[to, block * lanes : (block + 1) * lanes] = lo


def transform_kernel(hi_ref, lo_ref, hist_ref, out_ref):
    hist = hist_ref[...].reshape(STEPS, 128)
    total = nn(hi_ref[...], hist) + nn(lo_ref[...], hist)
    out_ref[...] = total.astype(BF16).reshape(out_ref.shape)


def signs(shape):
    lane = lax.broadcasted_iota(jnp.int32, shape, len(shape) - 1)
    return jnp.where(lane < 64, -1.0, 1.0).astype(F32)


def coeff_kernel(recv_ref, basis_ref, dens_ref, coef_ref):
    waves = 32
    turned = jnp.swapaxes(recv_ref[...].astype(F32), 0, 1).reshape(2, waves, 8, 128)
    dens_ref[...] = jnp.swapaxes(turned, 0, 1).reshape(waves, 16, 128).astype(BF16)
    lane = lax.broadcasted_iota(jnp.int32, (32, 128), 1)
    lane_wave = (lane >> 3) & 7
    for group in range(waves // 8):
        right = turned[:, 8 * group : 8 * group + 8].reshape(128, 128).astype(BF16)
        left = basis_ref[8 * group : 8 * group + 8].reshape(512, 128)
        out = nt(left, right).reshape(8, 2, 32, 128)
        by_re = jnp.zeros((32, 128), F32)
        by_im = jnp.zeros((32, 128), F32)
        for wave in range(8):
            by_re = jnp.where(lane_wave == wave, out[wave, 0], by_re)
            by_im = jnp.where(lane_wave == wave, out[wave, 1], by_im)
        value = by_re + signs((32, 128)) * pltpu.roll(by_im, 64, 1)
        coef_ref[group * 32 : (group + 1) * 32] = value.astype(BF16)


def mask_kernel(mine_ref, ranks_ref, couple_ref, out_ref):
    waves, clusters, rank = ranks_ref.shape[0], ranks_ref.shape[1], couple_ref.shape[2]
    wide = clusters * rank
    ids = lax.broadcasted_iota(jnp.int32, (waves, clusters), 1)
    limit = ranks_ref[...]
    for slot in range(4):
        limit = jnp.where(ids == mine_ref[slot], 0, limit)
    row = lax.broadcasted_iota(jnp.int32, (clusters, wide), 0)
    col = lax.broadcasted_iota(jnp.int32, (clusters, wide), 1)
    spread = jnp.where((col >> 5) == row, 1.0, 0.0).astype(BF16)
    limits = nn(limit.astype(F32).astype(BF16), spread)
    inner = (lax.broadcasted_iota(jnp.int32, (waves, wide), 1) & 31).astype(F32)
    limits = jnp.where(inner < limits, limits, 0.0)
    outer = lax.broadcasted_iota(jnp.int32, (rank, wide), 0).astype(F32)
    for wave in range(waves):
        keep = outer < limits[wave : wave + 1]
        for part in range(2):
            block = couple_ref[wave, part].astype(F32)
            out_ref[wave, part] = jnp.where(keep, block, 0.0).astype(BF16)


def near_kernel(mine_ref, me_ref, blocks_ref, *refs):
    own_ref, moved_refs, out_ref = refs[0], refs[1:-1], refs[-1]
    waves = own_ref.shape[0]
    sources = [own_ref[...]]
    for slot in range(1, 4):
        offset = mine_ref[slot] - me_ref[0]
        picked = moved_refs[0][...]
        for moved, distance in zip(moved_refs[1:], OFFSETS[1:]):
            from_there = lax.rem(offset + distance + 32, 16) == 0
            picked = jnp.where(from_there, moved[...], picked)
        sources.append(picked)
    for wave in range(waves):
        total = nt(sources[0][wave], blocks_ref[0, wave].reshape(256, 128))
        for slot in range(1, 4):
            total += nt(sources[slot][wave], blocks_ref[slot, wave].reshape(256, 128))
        out_ref[wave, 0:8] = total[0:8, 0:128] - total[8:16, 128:256]
        out_ref[wave, 8:16] = total[8:16, 0:128] + total[0:8, 128:256]


def far_kernel(all_ref, couple_ref, basis_ref, near_ref, out_ref):
    row_wave = lax.broadcasted_iota(jnp.int32, (8, 32, 128), 0)
    lane_wave = (lax.broadcasted_iota(jnp.int32, (8, 32, 128), 2) >> 3) & 7
    same = row_wave == lane_wave
    sign = signs((256, 128))
    for group in range(4):
        waves = slice(8 * group, 8 * group + 8)
        right = all_ref[:, group * 32 : (group + 1) * 32].reshape(512, 128)
        left = couple_ref[waves].reshape(512, 512)
        out = nn(left, right).reshape(8, 2, 32, 128)
        by_re = out[:, 0].reshape(256, 128)
        by_im = out[:, 1].reshape(256, 128)
        mixed = by_re + sign * pltpu.roll(by_im, 64, 1)
        mixed = jnp.where(same.reshape(256, 128), mixed, 0.0).astype(BF16).astype(F32)
        turned = (sign * pltpu.roll(mixed, 64, 1)).astype(BF16)
        mixed = mixed.astype(BF16)
        basis_re = basis_ref[waves, 0].reshape(256, 128)
        basis_im = basis_ref[waves, 1].reshape(256, 128)
        far = tn(mixed, basis_re) + tn(turned, basis_im)
        far = jnp.swapaxes(far.reshape(2, 8, 8, 128), 0, 1).reshape(8, 16, 128)
        out_ref[waves] = (far + near_ref[waves]).astype(BF16)


def local(history, near_blocks, near_list, basis_out, basis_in, coupling, ranks):
    me = lax.axis_index("clus").astype(jnp.int32)
    mine = lax.dynamic_index_in_dim(near_list, me, 0, keepdims=False)
    half = (lax.axis_index("freq") // 8).astype(jnp.int32).reshape(1)
    smem = pl.BlockSpec(memory_space=pltpu.SMEM)
    vmem = pl.BlockSpec(memory_space=VMEM)
    groups = [list(range(8)), list(range(8, 16))]

    packed = pl.pallas_call(
        pack_kernel, out_shape=jax.ShapeDtypeStruct((16, 64, 128), BF16), compiler_params=params()
    )(history)
    mixed_in = lax.all_to_all(packed, "freq", 0, 0, tiled=True)
    hi, lo = pl.pallas_call(
        table_kernel,
        in_specs=[smem],
        out_shape=[jax.ShapeDtypeStruct((512, STEPS), BF16)] * 2,
        scratch_shapes=[VMEM((256, 128), F32)] * 2,
        compiler_params=params(),
    )(half)
    masked = pl.pallas_call(
        mask_kernel,
        in_specs=[smem, vmem, vmem],
        out_shape=jax.ShapeDtypeStruct((32, 2, 32, 512), BF16),
        compiler_params=params(),
    )(mine, ranks[0], coupling[0])
    spectrum = pl.pallas_call(
        transform_kernel, out_shape=jax.ShapeDtypeStruct((8, 64, 128), BF16), compiler_params=params()
    )(hi, lo, mixed_in)
    received = lax.all_to_all(spectrum, "freq", 0, 0, tiled=True, axis_index_groups=groups)
    dens, coeffs = pl.pallas_call(
        coeff_kernel,
        out_shape=[jax.ShapeDtypeStruct((32, 16, 128), BF16), jax.ShapeDtypeStruct((128, 128), BF16)],
        compiler_params=params(),
    )(received, basis_in)
    moved = [from_behind(dens, "clus", distance) for distance in OFFSETS]
    wide = jnp.broadcast_to(coeffs[None], (16, 128, 128))
    everyone = lax.all_to_all(wide, "clus", 0, 0, tiled=True)
    step = 4
    source = pl.BlockSpec((step, 16, 128), lambda i: (i, 0, 0))
    near = pl.pallas_call(
        near_kernel,
        grid=(32 // step,),
        in_specs=[smem, smem, pl.BlockSpec((4, step, 2, 128, 128), lambda i: (0, i, 0, 0, 0))] + [source] * 7,
        out_specs=pl.BlockSpec((step, 16, 128), lambda i: (i, 0, 0)),
        out_shape=jax.ShapeDtypeStruct((32, 16, 128), F32),
        compiler_params=params(),
    )(mine, me.reshape(1), near_blocks[0], dens, *moved)
    out = pl.pallas_call(
        far_kernel, out_shape=jax.ShapeDtypeStruct((32, 16, 128), BF16), compiler_params=params()
    )(everyone, masked, basis_out, near)
    return out.reshape(32, 2, 8, 128)


def solution(mesh):
    placed = (
        P("freq", None, "clus"),
        P("clus", None, "freq", None, None, None),
        P(),
        P("freq", None, None, "clus"),
        P("freq", None, None, "clus"),
        P("clus", "freq", None, None, None),
        P("clus", "freq", None),
    )
    return jax.shard_map(
        local, mesh=mesh, in_specs=placed, out_specs=P("freq", None, None, "clus"), check_vma=False
    )
```

```python
import math

import jax
import jax.numpy as jnp
from jax import lax
from jax.experimental import pallas as pl
from jax.experimental.pallas import tpu as pltpu
from jax.sharding import PartitionSpec as P

STEPS = 1024
F32 = jnp.float32
BF16 = jnp.bfloat16
VMEM = pltpu.VMEM
FROM_EVEN = (1, -2, 2, -1, 3, -3)
FROM_ODD = (-1, -2, 2, -3, 1, 3)


def params(mib=12):
    return pltpu.CompilerParams(vmem_limit_bytes=mib * 1024 * 1024)


def nt(a, b):
    return lax.dot_general(a, b, (((1,), (1,)), ((), ())), preferred_element_type=F32)


def nn(a, b):
    return lax.dot_general(a, b, (((1,), (0,)), ((), ())), preferred_element_type=F32)


def tn(a, b):
    return lax.dot_general(a, b, (((0,), (0,)), ((), ())), preferred_element_type=F32)


def from_behind(block, axis, distance):
    devices = range(lax.axis_size(axis))
    route = [((i - distance) % len(devices), i) for i in devices]
    return lax.ppermute(block, axis, route)


def pack_kernel(hist_ref, out_ref):
    exc = hist_ref.shape[1]
    slabs = jnp.swapaxes(hist_ref[...].astype(F32), 0, 1).astype(BF16)
    for copy in range(out_ref.shape[0] // exc):
        out_ref[copy * exc : (copy + 1) * exc] = slabs


def fill_table(half, hi_ref, lo_ref, base_c, base_s):
    dests, waves, lanes = 8, 32, 128
    count = dests * waves
    first = half * count
    wave = first + lax.broadcasted_iota(jnp.int32, (count, lanes), 0)
    step = lax.broadcasted_iota(jnp.int32, (count, lanes), 1)
    theta = lax.rem(wave * step, STEPS).astype(F32) * (2.0 * math.pi / STEPS)
    weight = jnp.exp(step.astype(F32) * (-math.log(2.0) / STEPS)) * STEPS ** (-0.5)
    base_c[...] = weight * jnp.cos(theta)
    base_s[...] = weight * jnp.sin(theta)
    sub = lax.broadcasted_iota(jnp.int32, (8, lanes), 0)
    for block in range(STEPS // lanes):
        gain = 2.0 ** (-block * lanes / STEPS)
        for part in range(2):
            phi = ((sub * block + 2 * part) & 7).astype(F32) * (math.pi / 4.0)
            turn_c = (gain * jnp.cos(phi))[None]
            turn_s = (gain * jnp.sin(phi))[None]
            for dest in range(dests):
                rows = slice(dest * waves, (dest + 1) * waves)
                tc = base_c[rows].reshape(waves // 8, 8, lanes)
                ts = base_s[rows].reshape(waves // 8, 8, lanes)
                value = (tc * turn_c - ts * turn_s).reshape(waves, lanes)
                hi = value.astype(BF16)
                lo = (value - hi.astype(F32)).astype(BF16)
                to = slice((dest * 2 + part) * waves, (dest * 2 + part + 1) * waves)
                hi_ref[to, block * lanes : (block + 1) * lanes] = hi
                lo_ref[to, block * lanes : (block + 1) * lanes] = lo


def transform_kernel(hi_ref, lo_ref, hist_ref, out_ref):
    hist = hist_ref[...].reshape(STEPS, 128)
    total = nn(hi_ref[...], hist) + nn(lo_ref[...], hist)
    out_ref[...] = total.astype(BF16).reshape(out_ref.shape)


def signs(shape):
    lane = lax.broadcasted_iota(jnp.int32, shape, len(shape) - 1)
    return jnp.where(lane < 64, -1.0, 1.0).astype(F32)


def fill_masked(mine, ranks_ref, couple_ref, out_ref):
    clusters, waves = ranks_ref.shape
    rank, wide = couple_ref.shape[2], couple_ref.shape[3]
    ids = lax.broadcasted_iota(jnp.int32, (clusters, waves), 0)
    limit = ranks_ref[...]
    for shard in mine:
        limit = jnp.where(ids == shard, 0, limit)
    row = lax.broadcasted_iota(jnp.int32, (clusters, wide), 0)
    col = lax.broadcasted_iota(jnp.int32, (clusters, wide), 1)
    spread = jnp.where((col >> 5) == row, 1.0, 0.0).astype(BF16)
    limits = tn(limit.astype(F32).astype(BF16), spread)
    inner = (lax.broadcasted_iota(jnp.int32, (waves, wide), 1) & 31).astype(F32)
    limits = jnp.where(inner < limits, limits, 0.0)
    outer = lax.broadcasted_iota(jnp.int32, (rank, wide), 0).astype(F32)
    for wave in range(waves):
        keep = outer < limits[wave : wave + 1]
        for part in range(2):
            block = couple_ref[wave, part].astype(F32)
            out_ref[wave, part] = jnp.where(keep, block, 0.0).astype(BF16)


def table_kernel(info_ref, hi_ref, lo_ref, base_c, base_s):
    fill_table(info_ref[5], hi_ref, lo_ref, base_c, base_s)


def mask_kernel(info_ref, ranks_ref, couple_hbm, masked_ref, couple_ref, sem):
    copy = pltpu.make_async_copy(couple_hbm, couple_ref, sem)
    copy.start()
    copy.wait()
    fill_masked([info_ref[slot] for slot in range(4)], ranks_ref, couple_ref, masked_ref)


def turn_kernel(basis_ref, turned_ref):
    for group in range(4):
        for part in range(2):
            basis = basis_ref[8 * group : 8 * group + 8, part].reshape(256, 128)
            turned_ref[group, :, part * 256 : (part + 1) * 256] = basis.astype(F32).T.astype(BF16)


def fetch_kernel(from_hbm, to_ref, sem):
    copy = pltpu.make_async_copy(from_hbm, to_ref, sem)
    copy.start()
    copy.wait()


def coeff_kernel(recv_ref, basis_ref, masked_ref, turned_ref, dens_ref, coef_ref):
    waves = 32
    rows = jnp.swapaxes(recv_ref[...].astype(F32), 0, 1).reshape(2, waves, 8, 128)
    lane = lax.broadcasted_iota(jnp.int32, (32, 128), 1)
    lane_wave = (lane >> 3) & 7
    sign = signs((32, 128))
    for group in range(waves // 8):
        right = rows[:, 8 * group : 8 * group + 8].reshape(128, 128).T.astype(BF16)
        dens_ref[group] = right
        left = basis_ref[8 * group : 8 * group + 8].reshape(512, 128)
        out = nn(left, right).reshape(8, 2, 32, 128)
        by_re = jnp.zeros((32, 128), F32)
        by_im = jnp.zeros((32, 128), F32)
        for wave in range(8):
            by_re = jnp.where(lane_wave == wave, out[wave, 0], by_re)
            by_im = jnp.where(lane_wave == wave, out[wave, 1], by_im)
        value = (by_re + sign * pltpu.roll(by_im, 64, 1)).astype(BF16)
        for copy in range(coef_ref.shape[0]):
            coef_ref[copy, group * 32 : (group + 1) * 32] = value


def near_product(blocks, dens):
    lane = lax.broadcasted_iota(jnp.int32, (128, 128), 1)
    lane_wave = (lane >> 3) & 7
    dens = dens.astype(F32)
    left = [blocks[wave].reshape(256, 128) for wave in range(8)]
    right = [jnp.where(lane_wave == wave, dens, 0.0).astype(BF16) for wave in range(8)]
    return nn(jnp.concatenate(left, 1), jnp.concatenate(right, 0))


def block_copies(blocks_hbm, blocks_ref, sems, slots):
    return [
        [
            pltpu.make_async_copy(
                blocks_hbm.at[slot, pl.ds(8 * group, 8)], blocks_ref.at[at, group], sems.at[at, group]
            )
            for at, slot in enumerate(slots)
        ]
        for group in range(4)
    ]


def near_own_kernel(blocks_hbm, own_ref, out_ref, blocks_ref, sems):
    copies = block_copies(blocks_hbm, blocks_ref, sems, [0])
    for group in range(4):
        copies[group][0].start()
    for group in range(4):
        copies[group][0].wait()
        out_ref[group] = near_product(blocks_ref[0, group], own_ref[group])


def near_rest_kernel(info_ref, blocks_hbm, first_ref, *refs):
    moved_refs, (out_ref, blocks_ref, sems) = refs[:-3], refs[-3:]
    copies = block_copies(blocks_hbm, blocks_ref, sems, [1, 2, 3])
    for group in range(4):
        for copy in copies[group]:
            copy.start()
    me = info_ref[4]
    even = (me & 1) == 0
    sign = signs((128, 128))
    for group in range(4):
        total = first_ref[group]
        for slot in range(1, 4):
            offset = info_ref[slot] - me
            picked = moved_refs[0][group]
            for moved, for_even, for_odd in zip(moved_refs[1:], FROM_EVEN[1:], FROM_ODD[1:]):
                there = lax.rem(offset - jnp.where(even, for_even, for_odd) + 32, 16) == 0
                picked = jnp.where(there, moved[group], picked)
            copies[group][slot - 1].wait()
            total += near_product(blocks_ref[slot - 1, group], picked)
        out_ref[group] = total[:128] + sign * pltpu.roll(total[128:], 64, 1)


def far_kernel(info_ref, mine_ref, other_ref, couple_ref, turned_ref, near_ref, out_ref):
    even_core = (info_ref[4] & 1) == 0
    row_wave = lax.broadcasted_iota(jnp.int32, (8, 32, 128), 0)
    lane_wave = (lax.broadcasted_iota(jnp.int32, (8, 32, 128), 2) >> 3) & 7
    same = (row_wave == lane_wave).reshape(256, 128)
    sign = signs((256, 128))
    for group in range(4):
        waves = slice(8 * group, 8 * group + 8)
        mine = mine_ref[:, group * 32 : (group + 1) * 32]
        other = other_ref[:, group * 32 : (group + 1) * 32]
        evens = jnp.where(even_core, mine, other)
        odds = jnp.where(even_core, other, mine)
        right = jnp.stack([evens, odds], 1).reshape(512, 128)
        out = nn(couple_ref[waves].reshape(512, 512), right).reshape(8, 2, 32, 128)
        by_re = out[:, 0].reshape(256, 128)
        by_im = out[:, 1].reshape(256, 128)
        mixed = by_re + sign * pltpu.roll(by_im, 64, 1)
        mixed = jnp.where(same, mixed, 0.0).astype(BF16)
        swapped = (sign * pltpu.roll(mixed.astype(F32), 64, 1)).astype(BF16)
        total = nn(turned_ref[group], jnp.concatenate([mixed, swapped], 0)) + near_ref[group]
        total = jnp.swapaxes(total.T.reshape(2, 8, 8, 128), 0, 1)
        out_ref[waves] = total.reshape(8, 16, 128).astype(BF16)


def partner(block):
    size = lax.axis_size("clus")
    return lax.ppermute(block, "clus", [(i, i ^ 1) for i in range(size)])


def cross(block):
    size = lax.axis_size("clus")
    return lax.ppermute(block, "clus", [(i, (i + 1 if i % 2 else i - 1) % size) for i in range(size)])


def call(kernel, outs, specs=None, scratch=()):
    return pl.pallas_call(
        kernel,
        in_specs=specs,
        out_shape=outs,
        scratch_shapes=list(scratch),
        compiler_params=params(),
    )


def local(history, near_blocks, near_list, basis_out, basis_in, coupling, ranks):
    shape = jax.ShapeDtypeStruct
    me = lax.axis_index("clus").astype(jnp.int32)
    half = (lax.axis_index("freq") >> 3).astype(jnp.int32)
    mine = lax.dynamic_index_in_dim(near_list, me, 0, keepdims=False)
    info = jnp.concatenate([mine, me[None], half[None]])
    smem = pl.BlockSpec(memory_space=pltpu.SMEM)
    vmem = pl.BlockSpec(memory_space=VMEM)
    hbm = pl.BlockSpec(memory_space=pltpu.HBM)
    groups = [list(range(8)), list(range(8, 16))]
    cores = [[2 * z + core for z in range(8)] for core in range(2)]

    packed = call(pack_kernel, shape((16, 64, 128), BF16), [vmem])(history)
    steps = lax.all_to_all(packed, "freq", 0, 0, tiled=True)
    couple, outer, inner_hbm, blocks_hbm = [
        pltpu.with_memory_space_constraint(a, pltpu.HBM) for a in (coupling[0], basis_out, basis_in, near_blocks[0])
    ]
    dma = pltpu.SemaphoreType.DMA
    masked = call(
        mask_kernel, shape((32, 2, 32, 512), BF16), [smem, vmem, hbm], [VMEM((32, 2, 32, 512), BF16), dma]
    )(info, ranks[0].T, couple)
    turned = call(turn_kernel, shape((4, 128, 512), BF16), [vmem])(basis_out)
    hi, lo = call(
        table_kernel, [shape((512, STEPS), BF16)] * 2, [smem], [VMEM((256, 128), F32)] * 2
    )(info)
    inner = call(fetch_kernel, shape(inner_hbm.shape, BF16), [hbm], [dma])(inner_hbm)
    spectrum = call(transform_kernel, shape((8, 64, 128), BF16), [vmem] * 3)(hi, lo, steps)
    received = lax.all_to_all(spectrum, "freq", 0, 0, tiled=True, axis_index_groups=groups)
    dens, coeffs = call(
        coeff_kernel, [shape((4, 128, 128), BF16), shape((8, 128, 128), BF16)], [vmem] * 4
    )(received, inner, masked, turned)
    same_core = lax.all_to_all(coeffs, "clus", 0, 0, tiled=True, axis_index_groups=cores)
    beside = partner(dens)
    behind = from_behind(dens, "clus", 2)
    ahead = from_behind(dens, "clus", -2)
    first = call(
        near_own_kernel,
        shape((4, 256, 128), F32),
        [hbm, vmem],
        [VMEM((1, 4, 8, 2, 128, 128), BF16), pltpu.SemaphoreType.DMA((1, 4))],
    )(blocks_hbm, dens)
    beyond = cross(jnp.where((me & 1) == 1, behind, ahead))
    moved = [beside, behind, ahead, partner(behind), partner(ahead), beyond]
    near = call(
        near_rest_kernel,
        shape((4, 128, 128), F32),
        [smem, hbm] + [vmem] * 7,
        [VMEM((3, 4, 8, 2, 128, 128), BF16), pltpu.SemaphoreType.DMA((3, 4))],
    )(info, blocks_hbm, first, *moved)
    other_core = partner(same_core)
    out = call(far_kernel, shape((32, 16, 128), BF16), [smem] + [vmem] * 5)(
        info, same_core, other_core, masked, turned, near
    )
    return out.reshape(32, 2, 8, 128)


def solution(mesh):
    placed = (
        P("freq", None, "clus"),
        P("clus", None, "freq", None, None, None),
        P(),
        P("freq", None, None, "clus"),
        P("freq", None, None, "clus"),
        P("clus", "freq", None, None, None),
        P("clus", "freq", None),
    )
    return jax.shard_map(
        local, mesh=mesh, in_specs=placed, out_specs=P("freq", None, None, "clus"), check_vma=False
    )
```

```python
import math

import jax
import jax.numpy as jnp
from jax import lax
from jax.experimental import pallas as pl
from jax.experimental.pallas import tpu as pltpu
from jax.sharding import PartitionSpec as P

STEPS = 1024
F32 = jnp.float32
BF16 = jnp.bfloat16
VMEM = pltpu.VMEM
FROM_EVEN = (1, -2, 2, -1, 3, -3)
FROM_ODD = (-1, -2, 2, -3, 1, 3)


def params(mib=12):
    return pltpu.CompilerParams(vmem_limit_bytes=mib * 1024 * 1024)


def nt(a, b):
    return lax.dot_general(a, b, (((1,), (1,)), ((), ())), preferred_element_type=F32)


def nn(a, b):
    return lax.dot_general(a, b, (((1,), (0,)), ((), ())), preferred_element_type=F32)


def tn(a, b):
    return lax.dot_general(a, b, (((0,), (0,)), ((), ())), preferred_element_type=F32)


def from_behind(block, axis, distance):
    devices = range(lax.axis_size(axis))
    route = [((i - distance) % len(devices), i) for i in devices]
    return lax.ppermute(block, axis, route)


def pack_kernel(hist_ref, out_ref):
    exc = hist_ref.shape[1]
    slabs = jnp.swapaxes(hist_ref[...].astype(F32), 0, 1).astype(BF16)
    for copy in range(out_ref.shape[0] // exc):
        out_ref[copy * exc : (copy + 1) * exc] = slabs


def fill_table(half, hi_ref, lo_ref, base_c, base_s):
    dests, waves, lanes = 8, 32, 128
    count = dests * waves
    first = half * count
    wave = first + lax.broadcasted_iota(jnp.int32, (count, lanes), 0)
    step = lax.broadcasted_iota(jnp.int32, (count, lanes), 1)
    theta = lax.rem(wave * step, STEPS).astype(F32) * (2.0 * math.pi / STEPS)
    weight = jnp.exp(step.astype(F32) * (-math.log(2.0) / STEPS)) * STEPS ** (-0.5)
    base_c[...] = weight * jnp.cos(theta)
    base_s[...] = weight * jnp.sin(theta)
    sub = lax.broadcasted_iota(jnp.int32, (8, lanes), 0)
    for block in range(STEPS // lanes):
        gain = 2.0 ** (-block * lanes / STEPS)
        for part in range(2):
            phi = ((sub * block + 2 * part) & 7).astype(F32) * (math.pi / 4.0)
            turn_c = (gain * jnp.cos(phi))[None]
            turn_s = (gain * jnp.sin(phi))[None]
            for dest in range(dests):
                rows = slice(dest * waves, (dest + 1) * waves)
                tc = base_c[rows].reshape(waves // 8, 8, lanes)
                ts = base_s[rows].reshape(waves // 8, 8, lanes)
                value = (tc * turn_c - ts * turn_s).reshape(waves, lanes)
                hi = value.astype(BF16)
                lo = (value - hi.astype(F32)).astype(BF16)
                to = slice((dest * 2 + part) * waves, (dest * 2 + part + 1) * waves)
                hi_ref[to, block * lanes : (block + 1) * lanes] = hi
                lo_ref[to, block * lanes : (block + 1) * lanes] = lo


def transform_kernel(hi_ref, lo_ref, hist_ref, basis_ref, out_ref):
    hist = hist_ref[...].reshape(STEPS, 128)
    total = nn(hi_ref[...], hist) + nn(lo_ref[...], hist)
    out_ref[...] = total.astype(BF16).reshape(out_ref.shape)


def signs(shape):
    lane = lax.broadcasted_iota(jnp.int32, shape, len(shape) - 1)
    return jnp.where(lane < 64, -1.0, 1.0).astype(F32)


def mask_limits(mine, ranks_ref):
    clusters, waves = ranks_ref.shape
    rank, wide = 32, 512
    ids = lax.broadcasted_iota(jnp.int32, (clusters, waves), 0)
    limit = ranks_ref[...]
    for shard in mine:
        limit = jnp.where(ids == shard, 0, limit)
    row = lax.broadcasted_iota(jnp.int32, (clusters, wide), 0)
    col = lax.broadcasted_iota(jnp.int32, (clusters, wide), 1)
    spread = jnp.where((col >> 5) == row, 1.0, 0.0).astype(BF16)
    limits = tn(limit.astype(F32).astype(BF16), spread)
    inner = (lax.broadcasted_iota(jnp.int32, (waves, wide), 1) & 31).astype(F32)
    outer = lax.broadcasted_iota(jnp.int32, (rank, wide), 0).astype(F32)
    return jnp.where(inner < limits, limits, 0.0), outer


def table_kernel(info_ref, masked_hbm, hi_ref, lo_ref, base_c, base_s):
    fill_table(info_ref[5], hi_ref, lo_ref, base_c, base_s)


def mask_kernel(info_ref, ranks_ref, couple_hbm, masked_hbm, couple_ref, masked_ref, sems):
    copies = [
        pltpu.make_async_copy(couple_hbm.at[pl.ds(8 * group, 8)], couple_ref.at[group], sems.at[0, group])
        for group in range(4)
    ]
    for copy in copies:
        copy.start()
    limits, outer = mask_limits([info_ref[slot] for slot in range(4)], ranks_ref)
    back = []
    for group in range(4):
        copies[group].wait()
        for wave in range(8):
            at = 8 * group + wave
            keep = outer < limits[at : at + 1]
            for part in range(2):
                block = couple_ref[group, wave, part].astype(F32)
                masked_ref[group, wave, part] = jnp.where(keep, block, 0.0).astype(BF16)
        back.append(
            pltpu.make_async_copy(masked_ref.at[group], masked_hbm.at[pl.ds(8 * group, 8)], sems.at[1, group])
        )
        back[-1].start()
    for copy in back:
        copy.wait()


def dens_kernel(recv_ref, dens_ref):
    rows = jnp.swapaxes(recv_ref[...].astype(F32), 0, 1).reshape(2, 32, 8, 128)
    for group in range(4):
        dens_ref[group] = rows[:, 8 * group : 8 * group + 8].reshape(128, 128).T.astype(BF16)


def coeff_kernel(dens_ref, basis_ref, coef_ref):
    lane = lax.broadcasted_iota(jnp.int32, (32, 128), 1)
    lane_wave = (lane >> 3) & 7
    sign = signs((32, 128))
    products = [
        nn(basis_ref[8 * group : 8 * group + 8].reshape(512, 128), dens_ref[group]).reshape(8, 2, 32, 128)
        for group in range(4)
    ]
    for group, out in enumerate(products):
        by_re = jnp.zeros((32, 128), F32)
        by_im = jnp.zeros((32, 128), F32)
        for wave in range(8):
            by_re = jnp.where(lane_wave == wave, out[wave, 0], by_re)
            by_im = jnp.where(lane_wave == wave, out[wave, 1], by_im)
        value = (by_re + sign * pltpu.roll(by_im, 64, 1)).astype(BF16)
        for copy in range(coef_ref.shape[0]):
            coef_ref[copy, group * 32 : (group + 1) * 32] = value


def near_product(blocks, dens):
    lane = lax.broadcasted_iota(jnp.int32, (128, 128), 1)
    lane_wave = (lane >> 3) & 7
    dens = dens.astype(F32)
    left = [blocks[wave].reshape(256, 128) for wave in range(8)]
    right = [jnp.where(lane_wave == wave, dens, 0.0).astype(BF16) for wave in range(8)]
    return nn(jnp.concatenate(left, 1), jnp.concatenate(right, 0))


def near_own_kernel(blocks_hbm, own_ref, basis_ref, out_ref, rest_ref, turned_ref, blocks_ref, sems):
    copies = [
        pltpu.make_async_copy(blocks_hbm.at[0, pl.ds(8 * group, 8)], blocks_ref.at[group], sems.at[group])
        for group in range(4)
    ]
    rest = pltpu.make_async_copy(blocks_hbm.at[pl.ds(1, 3)], rest_ref, sems.at[4])
    for copy in copies:
        copy.start()
    rest.start()
    for group in range(4):
        for part in range(2):
            basis = basis_ref[8 * group : 8 * group + 8, part].reshape(256, 128)
            turned_ref[group, :, part * 256 : (part + 1) * 256] = basis.astype(F32).T.astype(BF16)
    for group in range(4):
        copies[group].wait()
        out_ref[group] = near_product(blocks_ref[group], own_ref[group])
    rest.wait()


def final_kernel(info_ref, blocks_ref, first_ref, mine_ref, other_ref, couple_ref, turned_ref, *refs):
    moved_refs, out_ref = refs[:-1], refs[-1]
    me = info_ref[4]
    even_core = (me & 1) == 0
    row_wave = lax.broadcasted_iota(jnp.int32, (8, 32, 128), 0)
    lane_wave = (lax.broadcasted_iota(jnp.int32, (8, 32, 128), 2) >> 3) & 7
    same = (row_wave == lane_wave).reshape(256, 128)
    sign = signs((256, 128))
    products = []
    for group in range(4):
        mine = mine_ref[:, group * 32 : (group + 1) * 32]
        other = other_ref[:, group * 32 : (group + 1) * 32]
        evens = jnp.where(even_core, mine, other)
        odds = jnp.where(even_core, other, mine)
        right = jnp.stack([evens, odds], 1).reshape(512, 128)
        left = couple_ref[8 * group : 8 * group + 8].reshape(512, 512)
        products.append(nn(left, right).reshape(8, 2, 32, 128))
    pairs = []
    for out in products:
        by_re = out[:, 0].reshape(256, 128)
        by_im = out[:, 1].reshape(256, 128)
        mixed = by_re + sign * pltpu.roll(by_im, 64, 1)
        mixed = jnp.where(same, mixed, 0.0).astype(BF16)
        swapped = (sign * pltpu.roll(mixed.astype(F32), 64, 1)).astype(BF16)
        pairs.append(jnp.concatenate([mixed, swapped], 0))
    fars = [nn(turned_ref[group], pairs[group]) for group in range(4)]
    for group in range(4):
        near = first_ref[group]
        for slot in range(1, 4):
            offset = info_ref[slot] - me
            picked = moved_refs[0][group]
            for moved, for_even, for_odd in zip(moved_refs[1:], FROM_EVEN[1:], FROM_ODD[1:]):
                there = lax.rem(offset - jnp.where(even_core, for_even, for_odd) + 32, 16) == 0
                picked = jnp.where(there, moved[group], picked)
            near += near_product(blocks_ref[slot - 1, 8 * group : 8 * group + 8], picked)
        total = near[:128] + sign[:128] * pltpu.roll(near[128:], 64, 1) + fars[group]
        total = jnp.swapaxes(total.T.reshape(2, 8, 8, 128), 0, 1)
        out_ref[8 * group : 8 * group + 8] = total.reshape(8, 16, 128).astype(BF16)


def partner(block):
    size = lax.axis_size("clus")
    return lax.ppermute(block, "clus", [(i, i ^ 1) for i in range(size)])


def cross(block):
    size = lax.axis_size("clus")
    return lax.ppermute(block, "clus", [(i, (i + 1 if i % 2 else i - 1) % size) for i in range(size)])


def call(kernel, outs, specs, scratch=(), out_specs=None):
    given = {} if out_specs is None else {"out_specs": out_specs}
    return pl.pallas_call(
        kernel,
        in_specs=specs,
        **given,
        out_shape=outs,
        scratch_shapes=list(scratch),
        compiler_params=params(),
    )


def local(history, near_blocks, near_list, basis_out, basis_in, coupling, ranks):
    shape = jax.ShapeDtypeStruct
    me = lax.axis_index("clus").astype(jnp.int32)
    half = (lax.axis_index("freq") >> 3).astype(jnp.int32)
    mine = lax.dynamic_index_in_dim(near_list, me, 0, keepdims=False)
    info = jnp.concatenate([mine, me[None], half[None]])
    smem = pl.BlockSpec(memory_space=pltpu.SMEM)
    vmem = pl.BlockSpec(memory_space=VMEM)
    hbm = pl.BlockSpec(memory_space=pltpu.HBM)
    groups = [list(range(8)), list(range(8, 16))]
    cores = [[2 * z + core for z in range(8)] for core in range(2)]

    packed = call(pack_kernel, shape((16, 64, 128), BF16), [vmem])(history)
    steps = lax.all_to_all(packed, "freq", 0, 0, tiled=True)
    couple, blocks_hbm = [pltpu.with_memory_space_constraint(a, pltpu.HBM) for a in (coupling[0], near_blocks[0])]
    dma = pltpu.SemaphoreType.DMA
    masked = call(
        mask_kernel,
        pltpu.HBM((32, 2, 32, 512), BF16),
        [smem, vmem, hbm],
        [VMEM((4, 8, 2, 32, 512), BF16), VMEM((4, 8, 2, 32, 512), BF16), dma((2, 4))],
        hbm,
    )(info, ranks[0].T, couple)
    hi, lo = call(
        table_kernel, [shape((512, STEPS), BF16)] * 2, [smem, hbm], [VMEM((256, 128), F32)] * 2
    )(info, pltpu.with_memory_space_constraint(masked, pltpu.HBM))
    spectrum = call(transform_kernel, shape((8, 64, 128), BF16), [vmem] * 4)(hi, lo, steps, basis_in)
    received = lax.all_to_all(spectrum, "freq", 0, 0, tiled=True, axis_index_groups=groups)
    dens = call(dens_kernel, shape((4, 128, 128), BF16), [vmem])(received)
    beside = partner(dens)
    behind = from_behind(dens, "clus", 2)
    ahead = from_behind(dens, "clus", -2)
    coeffs = call(coeff_kernel, shape((8, 128, 128), BF16), [vmem] * 2)(dens, basis_in)
    same_core = lax.all_to_all(coeffs, "clus", 0, 0, tiled=True, axis_index_groups=cores)
    beyond = cross(jnp.where((me & 1) == 1, behind, ahead))
    first, rest, turned = call(
        near_own_kernel,
        [shape((4, 256, 128), F32), shape((3, 32, 2, 128, 128), BF16), shape((4, 128, 512), BF16)],
        [hbm] + [vmem] * 2,
        [VMEM((4, 8, 2, 128, 128), BF16), dma((5,))],
    )(blocks_hbm, dens, basis_out)
    moved = [beside, behind, ahead, partner(behind), partner(ahead), beyond]
    other_core = partner(same_core)
    out = call(final_kernel, shape((32, 16, 128), BF16), [smem] + [vmem] * 12)(
        info, rest, first, same_core, other_core, masked, turned, *moved
    )
    return out.reshape(32, 2, 8, 128)


def solution(mesh):
    placed = (
        P("freq", None, "clus"),
        P("clus", None, "freq", None, None, None),
        P(),
        P("freq", None, None, "clus"),
        P("freq", None, None, "clus"),
        P("clus", "freq", None, None, None),
        P("clus", "freq", None),
    )
    return jax.shard_map(
        local, mesh=mesh, in_specs=placed, out_specs=P("freq", None, None, "clus"), check_vma=False
    )
```

```python
import math

import jax
import jax.numpy as jnp
from jax import lax
from jax.experimental import pallas as pl
from jax.experimental.pallas import tpu as pltpu
from jax.sharding import PartitionSpec as P

STEPS = 1024
F32 = jnp.float32
BF16 = jnp.bfloat16
VMEM = pltpu.VMEM
FROM_EVEN = (1, -2, 2, -1, 3, -3)
FROM_ODD = (-1, -2, 2, -3, 1, 3)


def params(mib=12):
    return pltpu.CompilerParams(vmem_limit_bytes=mib * 1024 * 1024)


def nt(a, b):
    return lax.dot_general(a, b, (((1,), (1,)), ((), ())), preferred_element_type=F32)


def nn(a, b):
    return lax.dot_general(a, b, (((1,), (0,)), ((), ())), preferred_element_type=F32)


def tn(a, b):
    return lax.dot_general(a, b, (((0,), (0,)), ((), ())), preferred_element_type=F32)


def from_behind(block, axis, distance):
    devices = range(lax.axis_size(axis))
    route = [((i - distance) % len(devices), i) for i in devices]
    return lax.ppermute(block, axis, route)


def pack_kernel(hist_ref, out_ref):
    exc = hist_ref.shape[1]
    slabs = jnp.swapaxes(hist_ref[...].astype(F32), 0, 1).astype(BF16)
    for copy in range(out_ref.shape[0] // exc):
        out_ref[copy * exc : (copy + 1) * exc] = slabs


def fill_table(half, hi_ref, lo_ref, base_c, base_s):
    dests, waves, lanes = 8, 32, 128
    count = dests * waves
    first = half * count
    wave = first + lax.broadcasted_iota(jnp.int32, (count, lanes), 0)
    step = lax.broadcasted_iota(jnp.int32, (count, lanes), 1)
    theta = lax.rem(wave * step, STEPS).astype(F32) * (2.0 * math.pi / STEPS)
    weight = jnp.exp(step.astype(F32) * (-math.log(2.0) / STEPS)) * STEPS ** (-0.5)
    base_c[...] = weight * jnp.cos(theta)
    base_s[...] = weight * jnp.sin(theta)
    sub = lax.broadcasted_iota(jnp.int32, (8, lanes), 0)
    for block in range(STEPS // lanes):
        gain = 2.0 ** (-block * lanes / STEPS)
        for part in range(2):
            phi = ((sub * block + 2 * part) & 7).astype(F32) * (math.pi / 4.0)
            turn_c = (gain * jnp.cos(phi))[None]
            turn_s = (gain * jnp.sin(phi))[None]
            for dest in range(dests):
                rows = slice(dest * waves, (dest + 1) * waves)
                tc = base_c[rows].reshape(waves // 8, 8, lanes)
                ts = base_s[rows].reshape(waves // 8, 8, lanes)
                value = (tc * turn_c - ts * turn_s).reshape(waves, lanes)
                hi = value.astype(BF16)
                lo = (value - hi.astype(F32)).astype(BF16)
                to = slice((dest * 2 + part) * waves, (dest * 2 + part + 1) * waves)
                hi_ref[to, block * lanes : (block + 1) * lanes] = hi
                lo_ref[to, block * lanes : (block + 1) * lanes] = lo


def transform_kernel(hi_ref, lo_ref, hist_ref, basis_hbm, out_ref, basis_ref, sem):
    copy = pltpu.make_async_copy(basis_hbm, basis_ref, sem)
    copy.start()
    hist = hist_ref[...].reshape(STEPS, 128)
    total = nn(hi_ref[...], hist) + nn(lo_ref[...], hist)
    out_ref[...] = total.astype(BF16).reshape(out_ref.shape)
    copy.wait()


def signs(shape):
    lane = lax.broadcasted_iota(jnp.int32, shape, len(shape) - 1)
    return jnp.where(lane < 64, -1.0, 1.0).astype(F32)


def mask_limits(mine, ranks_ref):
    clusters, waves = ranks_ref.shape
    rank, wide = 32, 512
    ids = lax.broadcasted_iota(jnp.int32, (clusters, waves), 0)
    limit = ranks_ref[...]
    for shard in mine:
        limit = jnp.where(ids == shard, 0, limit)
    row = lax.broadcasted_iota(jnp.int32, (clusters, wide), 0)
    col = lax.broadcasted_iota(jnp.int32, (clusters, wide), 1)
    spread = jnp.where((col >> 5) == row, 1.0, 0.0).astype(BF16)
    limits = tn(limit.astype(F32).astype(BF16), spread)
    inner = (lax.broadcasted_iota(jnp.int32, (waves, wide), 1) & 31).astype(F32)
    outer = lax.broadcasted_iota(jnp.int32, (rank, wide), 0).astype(F32)
    return jnp.where(inner < limits, limits, 0.0), outer


def table_kernel(info_ref, hi_ref, lo_ref, base_c, base_s):
    fill_table(info_ref[5], hi_ref, lo_ref, base_c, base_s)


def mask_kernel(info_ref, ranks_hbm, couple_hbm, masked_ref, ranks_ref, couple_ref, sems):
    rank_copy = pltpu.make_async_copy(ranks_hbm, ranks_ref, sems.at[4])
    rank_copy.start()
    copies = [
        pltpu.make_async_copy(couple_hbm.at[pl.ds(8 * group, 8)], couple_ref.at[group], sems.at[group])
        for group in range(4)
    ]
    for copy in copies:
        copy.start()
    rank_copy.wait()
    limits, outer = mask_limits([info_ref[slot] for slot in range(4)], ranks_ref)
    for group in range(4):
        copies[group].wait()
        for wave in range(8):
            at = 8 * group + wave
            keep = outer < limits[at : at + 1]
            for part in range(2):
                block = couple_ref[group, wave, part].astype(F32)
                masked_ref[at, part] = jnp.where(keep, block, 0.0).astype(BF16)


def coeff_kernel(recv_ref, basis_ref, out_ref):
    rows = jnp.swapaxes(recv_ref[...].astype(F32), 0, 1).reshape(2, 32, 8, 128)
    lane = lax.broadcasted_iota(jnp.int32, (32, 128), 1)
    lane_wave = (lane >> 3) & 7
    sign = signs((32, 128))
    products = []
    for group in range(4):
        dens = rows[:, 8 * group : 8 * group + 8].reshape(128, 128).T.astype(BF16)
        out_ref[group] = dens
        left = basis_ref[8 * group : 8 * group + 8].reshape(512, 128)
        products.append(nn(left, dens).reshape(8, 2, 32, 128))
    for group, out in enumerate(products):
        by_re = jnp.zeros((32, 128), F32)
        by_im = jnp.zeros((32, 128), F32)
        for wave in range(8):
            by_re = jnp.where(lane_wave == wave, out[wave, 0], by_re)
            by_im = jnp.where(lane_wave == wave, out[wave, 1], by_im)
        value = (by_re + sign * pltpu.roll(by_im, 64, 1)).astype(BF16)
        out_ref[4, group * 32 : (group + 1) * 32] = value


def near_product(blocks, dens):
    lane = lax.broadcasted_iota(jnp.int32, (128, 128), 1)
    lane_wave = (lane >> 3) & 7
    dens = dens.astype(F32)
    left = [blocks[wave].reshape(256, 128) for wave in range(8)]
    right = [jnp.where(lane_wave == wave, dens, 0.0).astype(BF16) for wave in range(8)]
    return nn(jnp.concatenate(left, 1), jnp.concatenate(right, 0))


def near_own_kernel(
    blocks_hbm, own_ref, basis_hbm, block_ref,
    out_ref, rest_ref, turned_ref, blocks_ref, basis_ref, sems,
):
    copies = [
        pltpu.make_async_copy(blocks_hbm.at[0, pl.ds(8 * group, 8)], blocks_ref.at[group], sems.at[group])
        for group in range(4)
    ]
    rest = pltpu.make_async_copy(blocks_hbm.at[pl.ds(1, 3)], rest_ref, sems.at[4])
    bases = pltpu.make_async_copy(basis_hbm, basis_ref, sems.at[5])
    for copy in copies:
        copy.start()
    bases.start()
    rest.start()
    for group in range(4):
        copies[group].wait()
        out_ref[group] = near_product(blocks_ref[group], own_ref[group])
    bases.wait()
    for group in range(4):
        for part in range(2):
            basis = basis_ref[8 * group : 8 * group + 8, part].reshape(256, 128)
            turned_ref[group, :, part * 256 : (part + 1) * 256] = basis.astype(F32).T.astype(BF16)
    rest.wait()


def forward_kernel(info_ref, own_ref, behind_ref, ahead_ref, masked_ref, block_ref, picked_ref):
    block_ref[0] = own_ref[4]
    block_ref[1] = behind_ref[4]
    block_ref[2] = ahead_ref[4]
    picked_ref[...] = jnp.where((info_ref[4] & 1) == 1, behind_ref[:4], ahead_ref[:4])


def join_kernel(up_ref, down_ref, turned_ref, beyond_ref, out_ref):
    out_ref[0:3] = up_ref[...]
    out_ref[3:5] = down_ref[0:2]


def final_kernel(info_ref, blocks_ref, first_ref, couple_ref, turned_ref, own_ref, *refs):
    moved_refs, (up_ref, down_ref, joined_ref, out_ref, all_ref) = refs[:6], refs[6:]
    beside_ref, behind_ref, ahead_ref, other_behind_ref, other_ahead_ref = moved_refs[:5]
    me = info_ref[4]
    even_core = (me & 1) == 0
    chip, core = me >> 1, me & 1
    held = [
        (core, own_ref, behind_ref, ahead_ref, up_ref, down_ref, 0),
        (1 - core, beside_ref, other_behind_ref, other_ahead_ref, joined_ref, joined_ref, 3),
    ]
    for lane, at_chip, before, after, up, down, base in held:
        parts = [(0, at_chip, 4), (-1, before, 4), (1, after, 4), (-3, up, 0), (-4, up, 1), (-2, up, 2), (3, down, base), (2, down, base + 1)]
        for away, ref, index in parts:
            all_ref[(chip + away) & 7, lane] = ref[index]
    row_wave = lax.broadcasted_iota(jnp.int32, (8, 32, 128), 0)
    lane_wave = (lax.broadcasted_iota(jnp.int32, (8, 32, 128), 2) >> 3) & 7
    same = (row_wave == lane_wave).reshape(256, 128)
    sign = signs((256, 128))
    products = []
    for group in range(4):
        right = all_ref[:, :, group * 32 : (group + 1) * 32].reshape(512, 128)
        left = couple_ref[8 * group : 8 * group + 8].reshape(512, 512)
        products.append(nn(left, right).reshape(8, 2, 32, 128))
    pairs = []
    for out in products:
        by_re = out[:, 0].reshape(256, 128)
        by_im = out[:, 1].reshape(256, 128)
        mixed = by_re + sign * pltpu.roll(by_im, 64, 1)
        mixed = jnp.where(same, mixed, 0.0).astype(BF16)
        swapped = (sign * pltpu.roll(mixed.astype(F32), 64, 1)).astype(BF16)
        pairs.append(jnp.concatenate([mixed, swapped], 0))
    fars = [nn(turned_ref[group], pairs[group]) for group in range(4)]
    for group in range(4):
        near = first_ref[group]
        for slot in range(1, 4):
            offset = info_ref[slot] - me
            picked = moved_refs[0][group]
            for moved, for_even, for_odd in zip(moved_refs[1:], FROM_EVEN[1:], FROM_ODD[1:]):
                there = lax.rem(offset - jnp.where(even_core, for_even, for_odd) + 32, 16) == 0
                picked = jnp.where(there, moved[group], picked)
            near += near_product(blocks_ref[slot - 1, 8 * group : 8 * group + 8], picked)
        total = near[:128] + sign[:128] * pltpu.roll(near[128:], 64, 1) + fars[group]
        total = jnp.swapaxes(total.T.reshape(2, 8, 8, 128), 0, 1)
        out_ref[8 * group : 8 * group + 8] = total.reshape(8, 16, 128).astype(BF16)


def partner(block):
    size = lax.axis_size("clus")
    return lax.ppermute(block, "clus", [(i, i ^ 1) for i in range(size)])


def cross(block):
    size = lax.axis_size("clus")
    return lax.ppermute(block, "clus", [(i, (i + 1 if i % 2 else i - 1) % size) for i in range(size)])


def call(kernel, outs, specs, scratch=(), out_specs=None):
    given = {} if out_specs is None else {"out_specs": out_specs}
    return pl.pallas_call(
        kernel,
        in_specs=specs,
        **given,
        out_shape=outs,
        scratch_shapes=list(scratch),
        compiler_params=params(),
    )


def local(history, near_blocks, near_list, basis_out, basis_in, coupling, ranks):
    shape = jax.ShapeDtypeStruct
    me = lax.axis_index("clus").astype(jnp.int32)
    half = (lax.axis_index("freq") >> 3).astype(jnp.int32)
    mine = lax.dynamic_index_in_dim(near_list, me, 0, keepdims=False)
    info = jnp.concatenate([mine, me[None], half[None]])
    smem = pl.BlockSpec(memory_space=pltpu.SMEM)
    vmem = pl.BlockSpec(memory_space=VMEM)
    hbm = pl.BlockSpec(memory_space=pltpu.HBM)
    groups = [list(range(8)), list(range(8, 16))]

    dma = pltpu.SemaphoreType.DMA
    couple, blocks_hbm, ranks_hbm, outer, inner = [
        pltpu.with_memory_space_constraint(a, pltpu.HBM)
        for a in (coupling[0], near_blocks[0], ranks[0].T, basis_out, basis_in)
    ]
    packed = call(pack_kernel, shape((16, 64, 128), BF16), [vmem])(history)
    steps = lax.all_to_all(packed, "freq", 0, 0, tiled=True)
    masked = call(
        mask_kernel,
        shape((32, 2, 32, 512), BF16),
        [smem, hbm, hbm],
        [VMEM((16, 32), jnp.int32), VMEM((4, 8, 2, 32, 512), BF16), dma((5,))],
    )(info, ranks_hbm, couple)
    hi, lo = call(
        table_kernel, [shape((512, STEPS), BF16)] * 2, [smem], [VMEM((256, 128), F32)] * 2
    )(info)
    spectrum, bases = call(
        transform_kernel,
        [shape((8, 64, 128), BF16), shape((32, 2, 32, 128), BF16)],
        [vmem] * 3 + [hbm],
        [dma],
    )(hi, lo, steps, inner)
    received = lax.all_to_all(spectrum, "freq", 0, 0, tiled=True, axis_index_groups=groups)
    packet = call(coeff_kernel, shape((5, 128, 128), BF16), [vmem] * 2)(received, bases)
    beside = partner(packet)
    behind = from_behind(packet, "clus", 2)
    ahead = from_behind(packet, "clus", -2)
    block, picked = call(
        forward_kernel, [shape((3, 128, 128), BF16), shape((4, 128, 128), BF16)], [smem] + [vmem] * 4
    )(info, packet, behind, ahead, masked)
    up = from_behind(block, "clus", 6)
    down = from_behind(block, "clus", -6)
    beyond = cross(picked)
    first, rest, turned = call(
        near_own_kernel,
        [
            shape((4, 256, 128), F32),
            shape((3, 32, 2, 128, 128), BF16),
            shape((4, 128, 512), BF16),
        ],
        [hbm, vmem, hbm, vmem],
        [VMEM((4, 8, 2, 128, 128), BF16), VMEM((32, 2, 32, 128), BF16), dma((6,))],
    )(blocks_hbm, packet, outer, block)
    joined = call(join_kernel, shape((5, 128, 128), BF16), [vmem] * 4)(up, down, turned, beyond)
    moved = [beside, behind, ahead, partner(behind), partner(ahead), beyond, up, down, partner(joined)]
    out = call(
        final_kernel,
        shape((32, 16, 128), BF16),
        [smem] + [vmem] * 14,
        [VMEM((8, 2, 128, 128), BF16)],
    )(info, rest, first, masked, turned, packet, *moved)
    return out.reshape(32, 2, 8, 128)


def solution(mesh):
    placed = (
        P("freq", None, "clus"),
        P("clus", None, "freq", None, None, None),
        P(),
        P("freq", None, None, "clus"),
        P("freq", None, None, "clus"),
        P("clus", "freq", None, None, None),
        P("clus", "freq", None),
    )
    return jax.shard_map(
        local, mesh=mesh, in_specs=placed, out_specs=P("freq", None, None, "clus"), check_vma=False
    )
```

```python
import math

import jax
import jax.numpy as jnp
from jax import lax
from jax.experimental import pallas as pl
from jax.experimental.pallas import tpu as pltpu
from jax.sharding import PartitionSpec as P

STEPS = 1024
F32 = jnp.float32
BF16 = jnp.bfloat16
VMEM = pltpu.VMEM
FROM_EVEN = (1, -2, 2, -1, 3, -3)
FROM_ODD = (-1, -2, 2, -3, 1, 3)


def params(mib=12):
    return pltpu.CompilerParams(vmem_limit_bytes=mib * 1024 * 1024)


def nt(a, b):
    return lax.dot_general(a, b, (((1,), (1,)), ((), ())), preferred_element_type=F32)


def nn(a, b):
    return lax.dot_general(a, b, (((1,), (0,)), ((), ())), preferred_element_type=F32)


def tn(a, b):
    return lax.dot_general(a, b, (((0,), (0,)), ((), ())), preferred_element_type=F32)


def from_behind(block, axis, distance):
    devices = range(lax.axis_size(axis))
    route = [((i - distance) % len(devices), i) for i in devices]
    return lax.ppermute(block, axis, route)


def pack_kernel(hist_ref, out_ref):
    exc = hist_ref.shape[1]
    slabs = jnp.swapaxes(hist_ref[...].astype(F32), 0, 1).astype(BF16)
    for copy in range(out_ref.shape[0] // exc):
        out_ref[copy * exc : (copy + 1) * exc] = slabs


def fill_table(half, hi_ref, lo_ref, base_c, base_s):
    dests, waves, lanes = 8, 32, 128
    count = dests * waves
    first = half * count
    wave = first + lax.broadcasted_iota(jnp.int32, (count, lanes), 0)
    step = lax.broadcasted_iota(jnp.int32, (count, lanes), 1)
    theta = lax.rem(wave * step, STEPS).astype(F32) * (2.0 * math.pi / STEPS)
    weight = jnp.exp(step.astype(F32) * (-math.log(2.0) / STEPS)) * STEPS ** (-0.5)
    base_c[...] = weight * jnp.cos(theta)
    base_s[...] = weight * jnp.sin(theta)
    sub = lax.broadcasted_iota(jnp.int32, (8, lanes), 0)
    for block in range(STEPS // lanes):
        gain = 2.0 ** (-block * lanes / STEPS)
        for part in range(2):
            phi = ((sub * block + 2 * part) & 7).astype(F32) * (math.pi / 4.0)
            turn_c = (gain * jnp.cos(phi))[None]
            turn_s = (gain * jnp.sin(phi))[None]
            for dest in range(dests):
                rows = slice(dest * waves, (dest + 1) * waves)
                tc = base_c[rows].reshape(waves // 8, 8, lanes)
                ts = base_s[rows].reshape(waves // 8, 8, lanes)
                value = (tc * turn_c - ts * turn_s).reshape(waves, lanes)
                hi = value.astype(BF16)
                lo = (value - hi.astype(F32)).astype(BF16)
                to = slice((dest * 2 + part) * waves, (dest * 2 + part + 1) * waves)
                hi_ref[to, block * lanes : (block + 1) * lanes] = hi
                lo_ref[to, block * lanes : (block + 1) * lanes] = lo


def transform_kernel(hi_ref, lo_ref, hist_ref, basis_ref, out_ref):
    hist = hist_ref[...].reshape(STEPS, 128)
    total = nn(hi_ref[...], hist) + nn(lo_ref[...], hist)
    out_ref[...] = total.astype(BF16).reshape(out_ref.shape)


def signs(shape):
    lane = lax.broadcasted_iota(jnp.int32, shape, len(shape) - 1)
    return jnp.where(lane < 64, -1.0, 1.0).astype(F32)


def mask_limits(mine, ranks_ref):
    clusters, waves = ranks_ref.shape
    rank, wide = 32, 512
    ids = lax.broadcasted_iota(jnp.int32, (clusters, waves), 0)
    limit = ranks_ref[...]
    for shard in mine:
        limit = jnp.where(ids == shard, 0, limit)
    row = lax.broadcasted_iota(jnp.int32, (clusters, wide), 0)
    col = lax.broadcasted_iota(jnp.int32, (clusters, wide), 1)
    spread = jnp.where((col >> 5) == row, 1.0, 0.0).astype(BF16)
    limits = tn(limit.astype(F32).astype(BF16), spread)
    inner = (lax.broadcasted_iota(jnp.int32, (waves, wide), 1) & 31).astype(F32)
    outer = lax.broadcasted_iota(jnp.int32, (rank, wide), 0).astype(F32)
    return jnp.where(inner < limits, limits, 0.0), outer


def table_kernel(info_ref, masked_hbm, hi_ref, lo_ref, base_c, base_s):
    fill_table(info_ref[5], hi_ref, lo_ref, base_c, base_s)


def mask_kernel(info_ref, ranks_hbm, couple_hbm, masked_hbm, ranks_ref, couple_ref, masked_ref, sems, rank_sem):
    rank_copy = pltpu.make_async_copy(ranks_hbm, ranks_ref, rank_sem)
    rank_copy.start()
    copies = [
        pltpu.make_async_copy(couple_hbm.at[pl.ds(8 * group, 8)], couple_ref.at[group], sems.at[0, group])
        for group in range(4)
    ]
    for copy in copies:
        copy.start()
    rank_copy.wait()
    limits, outer = mask_limits([info_ref[slot] for slot in range(4)], ranks_ref)
    back = []
    for group in range(4):
        copies[group].wait()
        for wave in range(8):
            at = 8 * group + wave
            keep = outer < limits[at : at + 1]
            for part in range(2):
                block = couple_ref[group, wave, part].astype(F32)
                masked_ref[group, wave, part] = jnp.where(keep, block, 0.0).astype(BF16)
        back.append(
            pltpu.make_async_copy(masked_ref.at[group], masked_hbm.at[pl.ds(8 * group, 8)], sems.at[1, group])
        )
        back[-1].start()
    for copy in back:
        copy.wait()


def dens_kernel(recv_ref, dens_ref):
    rows = jnp.swapaxes(recv_ref[...].astype(F32), 0, 1).reshape(2, 32, 8, 128)
    for group in range(4):
        dens_ref[group] = rows[:, 8 * group : 8 * group + 8].reshape(128, 128).T.astype(BF16)


def coeff_kernel(dens_ref, basis_ref, coef_ref):
    lane = lax.broadcasted_iota(jnp.int32, (32, 128), 1)
    lane_wave = (lane >> 3) & 7
    sign = signs((32, 128))
    products = [
        nn(basis_ref[8 * group : 8 * group + 8].reshape(512, 128), dens_ref[group]).reshape(8, 2, 32, 128)
        for group in range(4)
    ]
    for group, out in enumerate(products):
        by_re = jnp.zeros((32, 128), F32)
        by_im = jnp.zeros((32, 128), F32)
        for wave in range(8):
            by_re = jnp.where(lane_wave == wave, out[wave, 0], by_re)
            by_im = jnp.where(lane_wave == wave, out[wave, 1], by_im)
        value = (by_re + sign * pltpu.roll(by_im, 64, 1)).astype(BF16)
        for copy in range(coef_ref.shape[0]):
            coef_ref[copy, group * 32 : (group + 1) * 32] = value


def near_product(blocks, dens):
    lane = lax.broadcasted_iota(jnp.int32, (128, 128), 1)
    lane_wave = (lane >> 3) & 7
    dens = dens.astype(F32)
    left = [blocks[wave].reshape(256, 128) for wave in range(8)]
    right = [jnp.where(lane_wave == wave, dens, 0.0).astype(BF16) for wave in range(8)]
    return nn(jnp.concatenate(left, 1), jnp.concatenate(right, 0))


def near_own_kernel(blocks_hbm, own_ref, basis_ref, out_ref, rest_ref, turned_ref, blocks_ref, sems):
    copies = [
        pltpu.make_async_copy(blocks_hbm.at[0, pl.ds(8 * group, 8)], blocks_ref.at[group], sems.at[group])
        for group in range(4)
    ]
    rest = pltpu.make_async_copy(blocks_hbm.at[pl.ds(1, 3)], rest_ref, sems.at[4])
    for copy in copies:
        copy.start()
    rest.start()
    for group in range(4):
        for part in range(2):
            basis = basis_ref[8 * group : 8 * group + 8, part].reshape(256, 128)
            turned_ref[group, :, part * 256 : (part + 1) * 256] = basis.astype(F32).T.astype(BF16)
    for group in range(4):
        copies[group].wait()
        out_ref[group] = near_product(blocks_ref[group], own_ref[group])
    rest.wait()


def final_kernel(info_ref, blocks_ref, first_ref, mine_ref, other_ref, couple_ref, turned_ref, *refs):
    moved_refs, out_ref = refs[:-1], refs[-1]
    me = info_ref[4]
    even_core = (me & 1) == 0
    row_wave = lax.broadcasted_iota(jnp.int32, (8, 32, 128), 0)
    lane_wave = (lax.broadcasted_iota(jnp.int32, (8, 32, 128), 2) >> 3) & 7
    same = (row_wave == lane_wave).reshape(256, 128)
    sign = signs((256, 128))
    products = []
    for group in range(4):
        mine = mine_ref[:, group * 32 : (group + 1) * 32]
        other = other_ref[:, group * 32 : (group + 1) * 32]
        evens = jnp.where(even_core, mine, other)
        odds = jnp.where(even_core, other, mine)
        right = jnp.stack([evens, odds], 1).reshape(512, 128)
        left = couple_ref[8 * group : 8 * group + 8].reshape(512, 512)
        products.append(nn(left, right).reshape(8, 2, 32, 128))
    pairs = []
    for out in products:
        by_re = out[:, 0].reshape(256, 128)
        by_im = out[:, 1].reshape(256, 128)
        mixed = by_re + sign * pltpu.roll(by_im, 64, 1)
        mixed = jnp.where(same, mixed, 0.0).astype(BF16)
        swapped = (sign * pltpu.roll(mixed.astype(F32), 64, 1)).astype(BF16)
        pairs.append(jnp.concatenate([mixed, swapped], 0))
    fars = [nn(turned_ref[group], pairs[group]) for group in range(4)]
    for group in range(4):
        near = first_ref[group]
        for slot in range(1, 4):
            offset = info_ref[slot] - me
            picked = moved_refs[0][group]
            for moved, for_even, for_odd in zip(moved_refs[1:], FROM_EVEN[1:], FROM_ODD[1:]):
                there = lax.rem(offset - jnp.where(even_core, for_even, for_odd) + 32, 16) == 0
                picked = jnp.where(there, moved[group], picked)
            near += near_product(blocks_ref[slot - 1, 8 * group : 8 * group + 8], picked)
        total = near[:128] + sign[:128] * pltpu.roll(near[128:], 64, 1) + fars[group]
        total = jnp.swapaxes(total.T.reshape(2, 8, 8, 128), 0, 1)
        out_ref[8 * group : 8 * group + 8] = total.reshape(8, 16, 128).astype(BF16)


def partner(block):
    size = lax.axis_size("clus")
    return lax.ppermute(block, "clus", [(i, i ^ 1) for i in range(size)])


def cross(block):
    size = lax.axis_size("clus")
    return lax.ppermute(block, "clus", [(i, (i + 1 if i % 2 else i - 1) % size) for i in range(size)])


def call(kernel, outs, specs, scratch=(), out_specs=None):
    given = {} if out_specs is None else {"out_specs": out_specs}
    return pl.pallas_call(
        kernel,
        in_specs=specs,
        **given,
        out_shape=outs,
        scratch_shapes=list(scratch),
        compiler_params=params(),
    )


def local(history, near_blocks, near_list, basis_out, basis_in, coupling, ranks):
    shape = jax.ShapeDtypeStruct
    me = lax.axis_index("clus").astype(jnp.int32)
    half = (lax.axis_index("freq") >> 3).astype(jnp.int32)
    mine = lax.dynamic_index_in_dim(near_list, me, 0, keepdims=False)
    info = jnp.concatenate([mine, me[None], half[None]])
    smem = pl.BlockSpec(memory_space=pltpu.SMEM)
    vmem = pl.BlockSpec(memory_space=VMEM)
    hbm = pl.BlockSpec(memory_space=pltpu.HBM)
    groups = [list(range(8)), list(range(8, 16))]
    cores = [[2 * z + core for z in range(8)] for core in range(2)]

    packed = call(pack_kernel, shape((16, 64, 128), BF16), [vmem])(history)
    steps = lax.all_to_all(packed, "freq", 0, 0, tiled=True)
    couple, blocks_hbm, ranks_hbm = [
        pltpu.with_memory_space_constraint(a, pltpu.HBM) for a in (coupling[0], near_blocks[0], ranks[0].T)
    ]
    dma = pltpu.SemaphoreType.DMA
    masked = call(
        mask_kernel,
        pltpu.HBM((32, 2, 32, 512), BF16),
        [smem, hbm, hbm],
        [
            VMEM((16, 32), jnp.int32),
            VMEM((4, 8, 2, 32, 512), BF16),
            VMEM((4, 8, 2, 32, 512), BF16),
            dma((2, 4)),
            dma,
        ],
        hbm,
    )(info, ranks_hbm, couple)
    hi, lo = call(
        table_kernel, [shape((512, STEPS), BF16)] * 2, [smem, hbm], [VMEM((256, 128), F32)] * 2
    )(info, pltpu.with_memory_space_constraint(masked, pltpu.HBM))
    spectrum = call(transform_kernel, shape((8, 64, 128), BF16), [vmem] * 4)(hi, lo, steps, basis_in)
    received = lax.all_to_all(spectrum, "freq", 0, 0, tiled=True, axis_index_groups=groups)
    dens = call(dens_kernel, shape((4, 128, 128), BF16), [vmem])(received)
    beside = partner(dens)
    behind = from_behind(dens, "clus", 2)
    ahead = from_behind(dens, "clus", -2)
    coeffs = call(coeff_kernel, shape((8, 128, 128), BF16), [vmem] * 2)(dens, basis_in)
    same_core = lax.all_to_all(coeffs, "clus", 0, 0, tiled=True, axis_index_groups=cores)
    beyond = cross(jnp.where((me & 1) == 1, behind, ahead))
    first, rest, turned = call(
        near_own_kernel,
        [shape((4, 256, 128), F32), shape((3, 32, 2, 128, 128), BF16), shape((4, 128, 512), BF16)],
        [hbm] + [vmem] * 2,
        [VMEM((4, 8, 2, 128, 128), BF16), dma((5,))],
    )(blocks_hbm, dens, basis_out)
    moved = [beside, behind, ahead, partner(behind), partner(ahead), beyond]
    other_core = partner(same_core)
    out = call(final_kernel, shape((32, 16, 128), BF16), [smem] + [vmem] * 12)(
        info, rest, first, same_core, other_core, masked, turned, *moved
    )
    return out.reshape(32, 2, 8, 128)


def solution(mesh):
    placed = (
        P("freq", None, "clus"),
        P("clus", None, "freq", None, None, None),
        P(),
        P("freq", None, None, "clus"),
        P("freq", None, None, "clus"),
        P("clus", "freq", None, None, None),
        P("clus", "freq", None),
    )
    return jax.shard_map(
        local, mesh=mesh, in_specs=placed, out_specs=P("freq", None, None, "clus"), check_vma=False
    )
```
